32 devices in a mesh: groups: 2 (over x), cols: 8 (over z, y), rows: 2 (over core).
Axes of the slice: x: 2, y: 2, z: 4, core: 2. Of those that a mesh axis runs over, the one named last changes fastest.
Arguments:
- queries: bfloat16 [2048, 4, 128], P(('groups', 'cols'), 'rows'), parts along dimension 0, may hold values from -18 to 18
- keys: bfloat16 [2048, 4, 128], P(('groups', 'cols'), 'rows'), parts along dimension 0, may hold values from -12 to 12
- values: bfloat16 [2048, 4, 128], P(('groups', 'cols'), 'rows'), parts along dimension 0, may hold values from -6 to 6
- out_grad: bfloat16 [2048, 4, 128], P(('groups', 'cols'), 'rows'), parts along dimension 0, may hold values from -6 to 6
- key_mask: int32 [2048, 4], P(('groups', 'cols'), 'rows'), parts along dimension 0, may hold values 0 or 1
- bias: bfloat16 [4, 2048, 1024], P(None, ('groups', 'cols')), parts along dimension 1, may hold values from -6 to 6
Outputs:
- query_grad: bfloat16 [2048, 4, 128], P(('groups', 'cols'), 'rows'), parts along dimension 0
- key_grad: bfloat16 [2048, 4, 128], P(('groups', 'cols'), 'rows'), parts along dimension 0
- value_grad: bfloat16 [2048, 4, 128], P(('groups', 'cols'), 'rows'), parts along dimension 0
- bias_grad: bfloat16 [4, 2048, 1024], P('rows', ('groups', 'cols')), parts along dimension 1
The draws below stay inside these ranges and needn't reach their ends.
There are 2 independent parts, one for each index of `groups`. The reference program is written for one: setup_inputs(seed, part) draws one part's arguments, and reference() takes and returns one part's arrays. A program takes and returns all parts, laid end to end along the dimension named above; each array names one. Nothing has to cross between parts.
All inputs are finite; a program needn't handle non-finite values. No bound on the sum of `key_mask` on one device may be relied on, other than what follows from the above.
Results may differ from the reference program's by a relative error of at most 0.0085.
Values may be sent and summed in bfloat16 or wider, within the bound.
A program may use at most 64 MiB of HBM per device.

```python
import math
import jax
import jax.numpy as jnp
from jax import lax

HEADS = 4
HEAD_DIM = 32
CHANNELS = 128
RESIDUES = 1024
SLAB = 4


def key_field(key):
    key = jax.random.fold_in(key, 11)
    first_key = jax.random.fold_in(key, 0)
    third_key = jax.random.fold_in(key, 2)
    shape = (RESIDUES, SLAB, CHANNELS)
    gaussian = jnp.clip(jax.random.normal(first_key, shape, jnp.float32), -4.0, 4.0)
    row_scale = jnp.exp(jax.random.uniform(third_key, (RESIDUES, 1, 1), jnp.float32, math.log(0.3), math.log(3.0)))
    base = gaussian * row_scale
    aligned = base
    return aligned


def draw_keys(key, part):
    aligned = key_field(key)
    return aligned.astype(jnp.bfloat16)


def draw_queries(key, part):
    shape = (RESIDUES, SLAB, CHANNELS)
    key = jax.random.fold_in(key, 23)
    query_draw = jnp.clip(jax.random.normal(key, shape, jnp.float32), -4.0, 4.0)
    return query_draw.astype(jnp.bfloat16)


def set_ends(values, key, smallest, largest):
    index_at = [jax.random.randint(jax.random.fold_in(key, axis), (), 0, length) for axis, length in enumerate(values.shape)]
    widest = values.shape.index(max(values.shape))
    neighbour = index_at[:widest] + [(index_at[widest] + 1) % values.shape[widest]] + index_at[widest + 1:]
    return values.at[tuple(index_at)].set(smallest).at[tuple(neighbour)].set(largest)


def steps_of(rng, shape, cuts, low, top_value):
    factor_of = 1.0
    for axis_at, blocks in cuts:
        draws = jax.random.uniform(jax.random.fold_in(jax.random.fold_in(rng, 6), axis_at), (blocks,), jnp.float32, low / len(cuts), top_value / len(cuts))
        factor_of = factor_of * jnp.repeat(jnp.exp(draws), shape[axis_at] // blocks).reshape((-1,) + (1,) * (len(shape) - 1 - axis_at))
    return factor_of


def centred(own_key, shape, scale, reach, shards=(), kind=jnp.bfloat16):
    gain = steps_of(own_key, shape, shards, -0.22, 0.18) if shards else 1.0
    values = jax.random.normal(own_key, shape, jnp.float32) * scale * gain
    return jnp.minimum(jnp.maximum(values, -reach), reach).astype(kind)


def setup_inputs(seed: int = 0, part: int = 0) -> dict:
    arg_keys = jax.random.split(jax.random.key(seed), 7)
    own_keys = jax.random.split(jax.random.fold_in(arg_keys[6], part), 7)
    return {
        "queries": draw_queries(jax.random.fold_in(jax.random.fold_in(arg_keys[6], part), 71), part),
        "keys": draw_keys(jax.random.fold_in(jax.random.fold_in(arg_keys[6], part), 71), part),
        "values": centred(own_keys[2], (RESIDUES, SLAB, CHANNELS), 1.0, 6.0, ((0, 8), (1, 2))),
        "out_grad": centred(own_keys[3], (RESIDUES, SLAB, CHANNELS), 1.0, 6.0, ((0, 8), (1, 2))),
        "key_mask": set_ends((jax.random.randint(own_keys[4], (RESIDUES, SLAB), 0, 10) < 9).astype(jnp.int32), jax.random.fold_in(own_keys[4], 1), 0, 1),
        "bias": centred(own_keys[5], (HEADS, RESIDUES, RESIDUES), 1.0, 6.0, ((1, 8),)),
    }


def reference(queries, keys, values, out_grad, key_mask, bias):
    score_scale = HEAD_DIM ** -0.5
    bias_t = jnp.transpose(bias.astype(jnp.float32), (0, 2, 1))

    def split_heads(array):
        return array.astype(jnp.float32).reshape(RESIDUES, HEADS, HEAD_DIM)

    def one_column(bias_acc, inputs):
        query_col, key_col, value_col, grad_col, mask_col = inputs
        query_heads = split_heads(query_col)
        key_heads = split_heads(key_col)
        value_heads = split_heads(value_col)
        grad_heads = split_heads(grad_col)
        penalty = jnp.where(mask_col > 0, 0.0, -1e9).astype(jnp.float32)
        logits = jnp.einsum('ihd,khd->hik', query_heads, key_heads) * score_scale + bias_t + penalty[None, None, :]
        row_max = jnp.max(logits, axis=-1, keepdims=True)
        log_total = row_max + jnp.log(jnp.sum(jnp.exp(logits - row_max), axis=-1, keepdims=True))
        exact_probs = jnp.exp(logits - log_total)
        rounded_probs = lax.optimization_barrier(exact_probs.astype(jnp.bfloat16)).astype(jnp.float32)
        product = jnp.einsum('ihd,khd->hik', grad_heads, value_heads)
        inner_row = jnp.sum(exact_probs * product, axis=-1, keepdims=True)
        dscore = lax.optimization_barrier((exact_probs * (product - inner_row)).astype(jnp.bfloat16)).astype(jnp.float32)
        value_part = jnp.einsum('hik,ihd->khd', rounded_probs, grad_heads)
        query_part = jnp.einsum('hik,khd->ihd', dscore, key_heads) * score_scale
        key_part = jnp.einsum('hik,ihd->khd', dscore, query_heads) * score_scale
        bias_acc = bias_acc + jnp.transpose(dscore, (0, 2, 1))
        shaped = (query_part.reshape(RESIDUES, CHANNELS).astype(jnp.bfloat16),
                  key_part.reshape(RESIDUES, CHANNELS).astype(jnp.bfloat16),
                  value_part.reshape(RESIDUES, CHANNELS).astype(jnp.bfloat16))
        return bias_acc, shaped

    inputs = (jnp.swapaxes(queries, 0, 1), jnp.swapaxes(keys, 0, 1), jnp.swapaxes(values, 0, 1),
              jnp.swapaxes(out_grad, 0, 1), jnp.swapaxes(key_mask, 0, 1))
    start_acc = jnp.zeros((HEADS, RESIDUES, RESIDUES), jnp.float32)
    bias_acc, grads = lax.scan(one_column, start_acc, inputs)
    query_grad = jnp.swapaxes(grads[0], 0, 1)
    key_grad = jnp.swapaxes(grads[1], 0, 1)
    value_grad = jnp.swapaxes(grads[2], 0, 1)
    return query_grad, key_grad, value_grad, bias_acc.astype(jnp.bfloat16)
```

```python
import functools

import jax
import jax.numpy as jnp
from jax import lax
from jax.experimental import pallas as pl
from jax.experimental.pallas import tpu as pltpu
from jax.sharding import PartitionSpec as P

HEAD_DIM = 32
MESH = pl.DeviceIdType.MESH
F32 = jnp.float32
BF16 = jnp.bfloat16


def dot_nt(a, b):
    return lax.dot_general(a, b, (((1,), (1,)), ((), ())), preferred_element_type=F32)


def dot_nn(a, b):
    return lax.dot_general(a, b, (((1,), (0,)), ((), ())), preferred_element_type=F32)


def kernel(
    ncols,
    qdo_ref, kv_ref, mask_ref, bias_ref,
    qout_ref, kout_ref, vout_ref, bout_ref,
    qg, k4, k4t, v4, pen, e_ref, dp_ref, stat, stin, fin,
    p_ref, ds_ref, kacc, vacc, qpart, qacc, ysbuf, yin, zin, bown, bsend, brecv,
    zs_sem, ys_sem, g_sem, st_s, st_r, fin_s, fin_r, y_s, y_r, z_s, z_r, b_s, b_r,
):
    nz = ncols // 2
    scale = HEAD_DIM ** (-0.5)
    me = lax.axis_index("cols")
    core = lax.axis_index("rows")
    z = me // 2
    y = me % 2
    oy = 1 - y
    peer = z * 2 + oy
    n = kv_ref.shape[2]
    heads = 4

    def block_of(c):
        return pl.ds(pl.multiple_of(c * n, n), n)

    def slab(c):
        return qg.at[:, :, block_of(c), :]

    barrier = pltpu.get_barrier_semaphore()

    @pl.loop(1, ncols)
    def _(d):
        pl.semaphore_signal(barrier, inc=1, device_id={"cols": lax.rem(me + d, ncols)}, device_id_type=MESH)

    pl.semaphore_signal(barrier, inc=1, device_id={"rows": 1 - core}, device_id_type=MESH)

    qg[:, :, block_of(me), :] = qdo_ref[...]
    pl.semaphore_wait(barrier, ncols)

    def up_copy(c):
        return pltpu.make_async_remote_copy(
            src_ref=slab(c), dst_ref=slab(c), send_sem=zs_sem.at[0, c // 2], recv_sem=g_sem.at[c],
            device_id={"cols": me + 2}, device_id_type=MESH)

    def down_copy(c):
        return pltpu.make_async_remote_copy(
            src_ref=slab(c), dst_ref=slab(c), send_sem=zs_sem.at[1, c // 2], recv_sem=g_sem.at[c],
            device_id={"cols": me - 2}, device_id_type=MESH)

    def side_copy(c):
        return pltpu.make_async_remote_copy(
            src_ref=slab(c), dst_ref=slab(c), send_sem=ys_sem.at[c // 2], recv_sem=g_sem.at[c],
            device_id={"cols": peer}, device_id_type=MESH)

    def chain(zs, act):
        c = zs * 2 + y

        @pl.when(jnp.logical_and(zs <= z, z < nz - 1))
        def _():
            act(up_copy(c))

        @pl.when(jnp.logical_and(zs >= z, z > 0))
        def _():
            act(down_copy(c))

        act(side_copy(c))

    def start(copy):
        copy.start()

    chain(z, start)

    lane = lax.broadcasted_iota(jnp.int32, (n, 128), 1) // HEAD_DIM
    row = lax.broadcasted_iota(jnp.int32, (128, n), 0) // HEAD_DIM
    head_at = [lax.rem(hh + 2 * core, heads) for hh in range(heads)]
    for j in range(2):
        key = kv_ref[j, 0].astype(F32)
        val = kv_ref[j, 1].astype(F32)
        key_t = key.T
        for hh in range(heads):
            rows = slice(hh * n, (hh + 1) * n)
            k4[j, rows, :] = jnp.where(lane == head_at[hh], key, 0.0).astype(BF16)
            v4[j, rows, :] = jnp.where(lane == head_at[hh], val, 0.0).astype(BF16)
            k4t[j, :, rows] = jnp.where(row == head_at[hh], key_t, 0.0).astype(BF16)
        pen[j] = jnp.broadcast_to(
            jnp.where(mask_ref[:, j:j + 1] > 0, 0.0, -1000000000.0).astype(F32), (n, n))
    kacc[...] = jnp.zeros_like(kacc)
    vacc[...] = jnp.zeros_like(vacc)

    def stat_copy(c):
        return pltpu.make_async_remote_copy(
            src_ref=stat.at[c], dst_ref=stin.at[me], send_sem=st_s.at[c], recv_sem=st_r.at[me],
            device_id={"cols": c}, device_id_type=MESH)

    def forward(c):
        at = block_of(c)
        for j in range(2):
            x = dot_nt(k4[j], qg[j, 0, at, :])
            dp = dot_nt(v4[j], qg[j, 1, at, :])
            for hh in range(heads):
                rows = slice(hh * n, (hh + 1) * n)
                s = x[rows] * scale + bias_ref[head_at[hh], :, at].astype(F32) + pen[j]
                top = jnp.max(s, axis=0, keepdims=True)
                e = jnp.exp(s - top)
                e_ref[j, rows, at] = e
                dp_ref[j, rows, at] = dp[rows]
                r = j * heads + hh
                stat[c, 0, r:r + 1, :] = top
                stat[c, 1, r:r + 1, :] = jnp.sum(e, axis=0, keepdims=True)
                stat[c, 2, r:r + 1, :] = jnp.sum(e * dp[rows], axis=0, keepdims=True)

        @pl.when(c != me)
        def _():
            stat_copy(c).start()

    short = jnp.minimum(z, nz - 1 - z)
    side = jnp.where(z < nz - 1 - z, 1, -1)

    def z_at(k):
        t = (k + 1) // 2
        near = z + t * (1 - 2 * (k % 2))
        return jnp.where(k <= 2 * short, near, z + side * (k - short))

    def wait_block(c):
        side_copy(c).wait_recv()

    @pl.loop(0, nz)
    def _(k):
        zs = z_at(k)

        @pl.when(k > 0)
        def _():
            wait_block(zs * 2 + y)
            chain(zs, start)

        forward(zs * 2 + y)

        @pl.when(k > 0)
        def _():
            c = z_at(k - 1) * 2 + oy
            wait_block(c)
            forward(c)

    last = z_at(nz - 1) * 2 + oy
    wait_block(last)
    forward(last)

    stin[me] = stat[me]

    @pl.loop(1, ncols)
    def _(d):
        c = lax.rem(me + d, ncols)
        pltpu.make_async_remote_copy(
            src_ref=stat.at[c], dst_ref=stin.at[c], send_sem=st_s.at[c], recv_sem=st_r.at[c],
            device_id={"cols": c}, device_id_type=MESH).wait_recv()

    top = stin[0, 0]
    for c in range(1, ncols):
        top = jnp.maximum(top, stin[c, 0])
    total = jnp.zeros_like(top)
    for c in range(ncols):
        total = total + stin[c, 1] * jnp.exp(stin[c, 0] - top)
    lse = top + jnp.log(total)
    delta = jnp.zeros_like(top)
    for c in range(ncols):
        delta = delta + stin[c, 2] * jnp.exp(stin[c, 0] - lse)
    fin[me, 0] = lse
    fin[me, 1] = delta

    def fin_copy(c, slot):
        return pltpu.make_async_remote_copy(
            src_ref=fin.at[slot], dst_ref=fin.at[slot], send_sem=fin_s.at[c], recv_sem=fin_r.at[slot],
            device_id={"cols": c}, device_id_type=MESH)

    @pl.loop(1, ncols)
    def _(d):
        fin_copy(lax.rem(me + d, ncols), me).start()

    def y_copy(zt):
        return pltpu.make_async_remote_copy(
            src_ref=ysbuf.at[zt], dst_ref=yin.at[zt], send_sem=y_s.at[zt], recv_sem=y_r.at[zt],
            device_id={"cols": peer}, device_id_type=MESH)

    def z_copy(zt, slot):
        return pltpu.make_async_remote_copy(
            src_ref=yin.at[zt], dst_ref=zin.at[slot], send_sem=z_s.at[zt], recv_sem=z_r.at[slot],
            device_id={"cols": zt * 2 + y}, device_id_type=MESH)

    def b_copy(zt):
        return pltpu.make_async_remote_copy(
            src_ref=bsend.at[zt], dst_ref=brecv.at[zt], send_sem=b_s.at[zt], recv_sem=b_r.at[zt],
            device_id={"rows": 1 - core}, device_id_type=MESH)

    def wait_fin(c):
        @pl.when(c != me)
        def _():
            fin_copy(c, c).wait_recv()

    def pass_on(zt):
        y_copy(zt).wait_recv()
        yin[zt] = (qacc[zt] + yin[zt].astype(F32)).astype(BF16)
        z_copy(zt, z).start()

    half = 2 * n

    @pl.loop(1, nz + 1)
    def _(step):
        zt = lax.rem(z + step, nz)
        wait_fin(zt * 2)
        wait_fin(zt * 2 + 1)
        at = pl.ds(pl.multiple_of(zt * half, half), half)
        shift0 = jnp.exp(stat[zt * 2, 0] - fin[zt * 2, 0])
        shift1 = jnp.exp(stat[zt * 2 + 1, 0] - fin[zt * 2 + 1, 0])
        factor = jnp.concatenate([shift0, shift1], axis=1)
        inner = jnp.concatenate([fin[zt * 2, 1], fin[zt * 2 + 1, 1]], axis=1)
        for j in range(2):
            for hh in range(heads):
                rows = slice(hh * n, (hh + 1) * n)
                r = j * heads + hh
                p = e_ref[j, rows, at] * factor[r:r + 1]
                p_ref[j, rows, :] = p.astype(BF16)
                ds_ref[j, rows, :] = (p * (dp_ref[j, rows, at] - inner[r:r + 1])).astype(BF16)
            part_v = dot_nn(p_ref[j], qg[j, 1, at, :])
            part_k = dot_nn(ds_ref[j], qg[j, 0, at, :])
            pick_v = part_v[0:n]
            pick_k = part_k[0:n]
            for hh in range(1, heads):
                here = lane == head_at[hh]
                pick_v = jnp.where(here, part_v[hh * n:(hh + 1) * n], pick_v)
                pick_k = jnp.where(here, part_k[hh * n:(hh + 1) * n], pick_k)
            vacc[j] += pick_v
            kacc[j] += pick_k
            qpart[j] = dot_nn(k4t[j], ds_ref[j])
        ysbuf[zt] = qpart[:, :, pl.ds(pl.multiple_of(oy * n, n), n)].astype(BF16)
        y_copy(zt).start()
        qacc[zt] = qpart[:, :, pl.ds(pl.multiple_of(y * n, n), n)]
        mine = slice(0, 2 * n)
        theirs = slice(2 * n, 4 * n)
        bsend[zt] = (ds_ref[0, theirs, :].astype(F32) + ds_ref[1, theirs, :].astype(F32)).astype(BF16)
        b_copy(zt).start()
        bown[zt] = ds_ref[0, mine, :].astype(F32) + ds_ref[1, mine, :].astype(F32)

        @pl.when(step > 1)
        def _():
            pass_on(lax.rem(z + step - 1, nz))

    for j in range(2):
        kout_ref[j] = (kacc[j] * scale).astype(BF16)
        vout_ref[j] = vacc[j].astype(BF16)

    @pl.loop(1, nz + 1)
    def _(step):
        zt = lax.rem(z + step, nz)
        b_copy(zt).wait_recv()
        at = pl.ds(pl.multiple_of(zt * half, half), half)
        for hh in range(2):
            rows = slice(hh * n, (hh + 1) * n)
            bout_ref[hh, :, at] = (bown[zt, rows, :] + brecv[zt, rows, :].astype(F32)).astype(BF16)

    y_copy(z).wait_recv()
    qacc[z] += yin[z].astype(F32)

    @pl.loop(1, nz)
    def _(step):
        zt = lax.rem(z + nz - step, nz)
        z_copy(zt, zt).wait_recv()
        qacc[z] += zin[zt].astype(F32)

    for j in range(2):
        qout_ref[j] = (qacc[z, j].T * scale).astype(BF16)

    @pl.loop(0, nz)
    def _(zs):
        def sent(copy):
            copy.wait_send()

        chain(zs, sent)
        y_copy(zs).wait_send()
        b_copy(zs).wait_send()

        @pl.when(zs != z)
        def _():
            z_copy(zs, z).wait_send()

    @pl.loop(1, ncols)
    def _(d):
        c = lax.rem(me + d, ncols)
        stat_copy(c).wait_send()
        fin_copy(c, me).wait_send()


def body(queries, keys, values, out_grad, key_mask, bias):
    n, slab_here, channels = queries.shape
    ncols = lax.axis_size("cols")
    nz = ncols // 2
    total = bias.shape[2]

    def by_column(a, b):
        return jnp.transpose(jnp.stack([a, b]), (2, 0, 1, 3))

    qdo = by_column(queries, out_grad)
    kv = by_column(keys, values)
    vmem = pl.BlockSpec(memory_space=pltpu.VMEM)
    dma = pltpu.SemaphoreType.DMA
    rows4 = 4 * n
    outs = pl.pallas_call(
        functools.partial(kernel, ncols),
        out_shape=(
            jax.ShapeDtypeStruct((2, n, channels), BF16),
            jax.ShapeDtypeStruct((2, n, channels), BF16),
            jax.ShapeDtypeStruct((2, n, channels), BF16),
            jax.ShapeDtypeStruct((2, n, total), BF16),
        ),
        in_specs=[vmem] * 4,
        out_specs=(vmem,) * 4,
        scratch_shapes=[
            pltpu.VMEM((2, 2, total, channels), BF16),
            pltpu.VMEM((2, rows4, channels), BF16),
            pltpu.VMEM((2, channels, rows4), BF16),
            pltpu.VMEM((2, rows4, channels), BF16),
            pltpu.VMEM((2, n, n), F32),
            pltpu.VMEM((2, rows4, total), F32),
            pltpu.VMEM((2, rows4, total), F32),
            pltpu.VMEM((ncols, 3, 8, n), F32),
            pltpu.VMEM((ncols, 3, 8, n), F32),
            pltpu.VMEM((ncols, 2, 8, n), F32),
            pltpu.VMEM((2, rows4, 2 * n), BF16),
            pltpu.VMEM((2, rows4, 2 * n), BF16),
            pltpu.VMEM((2, n, channels), F32),
            pltpu.VMEM((2, n, channels), F32),
            pltpu.VMEM((2, channels, 2 * n), F32),
            pltpu.VMEM((nz, 2, channels, n), F32),
            pltpu.VMEM((nz, 2, channels, n), BF16),
            pltpu.VMEM((nz, 2, channels, n), BF16),
            pltpu.VMEM((nz, 2, channels, n), BF16),
            pltpu.VMEM((nz, 2 * n, 2 * n), F32),
            pltpu.VMEM((nz, 2 * n, 2 * n), BF16),
            pltpu.VMEM((nz, 2 * n, 2 * n), BF16),
            dma((2, nz)), dma((nz,)), dma((ncols,)),
            dma((ncols,)), dma((ncols,)), dma((ncols,)), dma((ncols,)),
            dma((nz,)), dma((nz,)), dma((nz,)), dma((nz,)), dma((nz,)), dma((nz,)),
        ],
        compiler_params=pltpu.CompilerParams(
            collective_id=0, has_side_effects=True, vmem_limit_bytes=60 * 1024 * 1024),
    )(qdo, kv, key_mask, bias)
    query_grad, key_grad, value_grad, bias_grad = outs

    def back(a):
        return jnp.transpose(a, (1, 0, 2))

    return (back(query_grad), back(key_grad), back(value_grad), bias_grad)


def solution(mesh):
    block = P(("groups", "cols"), "rows", None)
    return jax.shard_map(
        body,
        mesh=mesh,
        in_specs=(block, block, block, block, P(("groups", "cols"), "rows"), P(None, ("groups", "cols"), None)),
        out_specs=(block, block, block, P("rows", ("groups", "cols"), None)),
        check_vma=False,
    )
```

```python
import functools

import jax
import jax.numpy as jnp
from jax import lax
from jax.experimental import pallas as pl
from jax.experimental.pallas import tpu as pltpu
from jax.sharding import PartitionSpec as P

HEAD_DIM = 32
MESH = pl.DeviceIdType.MESH
F32 = jnp.float32
BF16 = jnp.bfloat16


def dot_nt(a, b):
    return lax.dot_general(a, b, (((1,), (1,)), ((), ())), preferred_element_type=F32)


def dot_nn(a, b):
    return lax.dot_general(a, b, (((1,), (0,)), ((), ())), preferred_element_type=F32)


def kernel(
    ncols,
    q_in, k_in, v_in, do_in, mask_ref, bias_hbm,
    qout_ref, kout_ref, vout_ref, bout_ref,
    qg, k4, k4t, v4, pen, e_ref, dp_ref, stat, stin, fin,
    p_ref, ds_ref, kacc, vacc, qpart, qacc, ysbuf, yin, zin, bown, bsend, brecv, bias_ref, wide,
    zs_sem, ys_sem, g_sem, st_s, st_r, fin_s, fin_r, y_s, y_r, z_s, z_r, b_s, b_r, in_s,
):
    nz = ncols // 2
    scale = HEAD_DIM ** (-0.5)
    me = lax.axis_index("cols")
    core = lax.axis_index("rows")
    z = me // 2
    y = me % 2
    oy = 1 - y
    peer = z * 2 + oy
    n = k_in.shape[0]
    heads = 4

    def block_of(c):
        return pl.ds(pl.multiple_of(c * n, n), n)

    def slab(c, j):
        return qg.at[j, :, block_of(c), :]

    def column(j):
        return wide[pl.ds(j, n, stride=2), :]

    barrier = pltpu.get_barrier_semaphore()

    @pl.loop(1, ncols)
    def _(d):
        pl.semaphore_signal(barrier, inc=1, device_id={"cols": lax.rem(me + d, ncols)}, device_id_type=MESH)

    pl.semaphore_signal(barrier, inc=1, device_id={"rows": 1 - core}, device_id_type=MESH)

    bias_copy = pltpu.make_async_copy(bias_hbm, bias_ref, in_s)
    bias_copy.start()
    for at_kind, source in enumerate((q_in, do_in)):
        wide[...] = source[...].astype(F32).reshape(2 * n, 128)
        for j in range(2):
            qg[j, at_kind, block_of(me), :] = column(j).astype(BF16)
    pl.semaphore_wait(barrier, ncols)

    def up_copy(c, j):
        return pltpu.make_async_remote_copy(
            src_ref=slab(c, j), dst_ref=slab(c, j), send_sem=zs_sem.at[0, c // 2, j], recv_sem=g_sem.at[c, j],
            device_id={"cols": me + 2}, device_id_type=MESH)

    def down_copy(c, j):
        return pltpu.make_async_remote_copy(
            src_ref=slab(c, j), dst_ref=slab(c, j), send_sem=zs_sem.at[1, c // 2, j], recv_sem=g_sem.at[c, j],
            device_id={"cols": me - 2}, device_id_type=MESH)

    def side_copy(c, j):
        return pltpu.make_async_remote_copy(
            src_ref=slab(c, j), dst_ref=slab(c, j), send_sem=ys_sem.at[c // 2, j], recv_sem=g_sem.at[c, j],
            device_id={"cols": peer}, device_id_type=MESH)

    def chain(zs, j, act):
        c = zs * 2 + y

        @pl.when(jnp.logical_and(zs <= z, z < nz - 1))
        def _():
            act(up_copy(c, j))

        @pl.when(jnp.logical_and(zs >= z, z > 0))
        def _():
            act(down_copy(c, j))

        act(side_copy(c, j))

    def start(copy):
        copy.start()

    for j in range(2):
        chain(z, j, start)

    lane = lax.broadcasted_iota(jnp.int32, (n, 128), 1) // HEAD_DIM
    row = lax.broadcasted_iota(jnp.int32, (128, n), 0) // HEAD_DIM
    head_at = [lax.rem(hh + 2 * core, heads) for hh in range(heads)]
    wide[...] = v_in[...].astype(F32).reshape(2 * n, 128)
    for j in range(2):
        val = column(j)
        for hh in range(heads):
            rows = slice(hh * n, (hh + 1) * n)
            v4[j, rows, :] = jnp.where(lane == head_at[hh], val, 0.0).astype(BF16)
    wide[...] = k_in[...].astype(F32).reshape(2 * n, 128)
    for j in range(2):
        key = column(j)
        key_t = key.T
        for hh in range(heads):
            rows = slice(hh * n, (hh + 1) * n)
            k4[j, rows, :] = jnp.where(lane == head_at[hh], key, 0.0).astype(BF16)
            k4t[j, :, rows] = jnp.where(row == head_at[hh], key_t, 0.0).astype(BF16)
        pen[j] = jnp.broadcast_to(
            jnp.where(mask_ref[j:j + 1, :] > 0, 0.0, -1000000000.0).astype(F32), (n, n)).T
    kacc[...] = jnp.zeros_like(kacc)
    vacc[...] = jnp.zeros_like(vacc)
    bias_copy.wait()

    def stat_copy(c):
        return pltpu.make_async_remote_copy(
            src_ref=stat.at[c], dst_ref=stin.at[me], send_sem=st_s.at[c], recv_sem=st_r.at[me],
            device_id={"cols": c}, device_id_type=MESH)

    def forward(c, j):
        at = block_of(c)
        x = dot_nt(k4[j], qg[j, 0, at, :])
        dp = dot_nt(v4[j], qg[j, 1, at, :])
        for hh in range(heads):
            rows = slice(hh * n, (hh + 1) * n)
            s = x[rows] * scale + bias_ref[head_at[hh], :, at].astype(F32) + pen[j]
            top = jnp.max(s, axis=0, keepdims=True)
            e = jnp.exp(s - top)
            e_ref[j, rows, at] = e
            dp_ref[j, rows, at] = dp[rows]
            r = j * heads + hh
            stat[c, 0, r:r + 1, :] = top
            stat[c, 1, r:r + 1, :] = jnp.sum(e, axis=0, keepdims=True)
            stat[c, 2, r:r + 1, :] = jnp.sum(e * dp[rows], axis=0, keepdims=True)

    short = jnp.minimum(z, nz - 1 - z)
    side = jnp.where(z < nz - 1 - z, 1, -1)

    def z_at(k):
        t = (k + 1) // 2
        near = z + t * (1 - 2 * (k % 2))
        return jnp.where(k <= 2 * short, near, z + side * (k - short))

    @pl.loop(0, nz)
    def _(k):
        zs = z_at(k)
        mine = zs * 2 + y
        other = z_at(k - 1) * 2 + oy
        for j in range(2):

            @pl.when(k > 0)
            def _():
                side_copy(mine, j).wait_recv()
                chain(zs, j, start)

            forward(mine, j)
            if j == 1:

                @pl.when(k > 0)
                def _():
                    stat_copy(mine).start()

            @pl.when(k > 0)
            def _():
                side_copy(other, j).wait_recv()
                forward(other, j)
                if j == 1:
                    stat_copy(other).start()

    last = z_at(nz - 1) * 2 + oy
    for j in range(2):
        side_copy(last, j).wait_recv()
        forward(last, j)
    stat_copy(last).start()

    stin[me] = stat[me]

    @pl.loop(1, ncols)
    def _(d):
        c = lax.rem(me + d, ncols)
        pltpu.make_async_remote_copy(
            src_ref=stat.at[c], dst_ref=stin.at[c], send_sem=st_s.at[c], recv_sem=st_r.at[c],
            device_id={"cols": c}, device_id_type=MESH).wait_recv()

    top = stin[0, 0]
    for c in range(1, ncols):
        top = jnp.maximum(top, stin[c, 0])
    total = jnp.zeros_like(top)
    for c in range(ncols):
        total = total + stin[c, 1] * jnp.exp(stin[c, 0] - top)
    lse = top + jnp.log(total)
    delta = jnp.zeros_like(top)
    for c in range(ncols):
        delta = delta + stin[c, 2] * jnp.exp(stin[c, 0] - lse)
    fin[me, 0] = lse
    fin[me, 1] = delta

    def fin_copy(c, slot):
        return pltpu.make_async_remote_copy(
            src_ref=fin.at[slot], dst_ref=fin.at[slot], send_sem=fin_s.at[c], recv_sem=fin_r.at[slot],
            device_id={"cols": c}, device_id_type=MESH)

    @pl.loop(1, ncols)
    def _(d):
        fin_copy(lax.rem(me + d, ncols), me).start()

    def y_copy(zt):
        return pltpu.make_async_remote_copy(
            src_ref=ysbuf.at[zt], dst_ref=yin.at[zt], send_sem=y_s.at[zt], recv_sem=y_r.at[zt],
            device_id={"cols": peer}, device_id_type=MESH)

    def z_copy(zt, slot):
        return pltpu.make_async_remote_copy(
            src_ref=yin.at[zt], dst_ref=zin.at[slot], send_sem=z_s.at[zt], recv_sem=z_r.at[slot],
            device_id={"cols": zt * 2 + y}, device_id_type=MESH)

    def b_copy(zt):
        return pltpu.make_async_remote_copy(
            src_ref=bsend.at[zt], dst_ref=brecv.at[zt], send_sem=b_s.at[zt], recv_sem=b_r.at[zt],
            device_id={"rows": 1 - core}, device_id_type=MESH)

    def wait_fin(c):
        @pl.when(c != me)
        def _():
            fin_copy(c, c).wait_recv()

    def pass_on(zt):
        y_copy(zt).wait_recv()
        yin[zt] = (qacc[zt] + yin[zt].astype(F32)).astype(BF16)
        z_copy(zt, z).start()

    half = 2 * n

    @pl.loop(1, nz + 1)
    def _(step):
        zt = lax.rem(z + step, nz)
        wait_fin(zt * 2)
        wait_fin(zt * 2 + 1)
        at = pl.ds(pl.multiple_of(zt * half, half), half)
        shift0 = jnp.exp(stat[zt * 2, 0] - fin[zt * 2, 0])
        shift1 = jnp.exp(stat[zt * 2 + 1, 0] - fin[zt * 2 + 1, 0])
        factor = jnp.concatenate([shift0, shift1], axis=1)
        inner = jnp.concatenate([fin[zt * 2, 1], fin[zt * 2 + 1, 1]], axis=1)
        for j in range(2):
            for hh in range(heads):
                rows = slice(hh * n, (hh + 1) * n)
                r = j * heads + hh
                p = e_ref[j, rows, at] * factor[r:r + 1]
                p_ref[j, rows, :] = p.astype(BF16)
                ds_ref[j, rows, :] = (p * (dp_ref[j, rows, at] - inner[r:r + 1])).astype(BF16)
            part_v = dot_nn(p_ref[j], qg[j, 1, at, :])
            part_k = dot_nn(ds_ref[j], qg[j, 0, at, :])
            pick_v = part_v[0:n]
            pick_k = part_k[0:n]
            for hh in range(1, heads):
                here = lane == head_at[hh]
                pick_v = jnp.where(here, part_v[hh * n:(hh + 1) * n], pick_v)
                pick_k = jnp.where(here, part_k[hh * n:(hh + 1) * n], pick_k)
            vacc[j] += pick_v
            kacc[j] += pick_k
            qpart[j] = dot_nn(k4t[j], ds_ref[j])
        ysbuf[zt] = qpart[:, :, pl.ds(pl.multiple_of(oy * n, n), n)].astype(BF16)
        y_copy(zt).start()
        qacc[zt] = qpart[:, :, pl.ds(pl.multiple_of(y * n, n), n)]
        mine = slice(0, 2 * n)
        theirs = slice(2 * n, 4 * n)
        bsend[zt] = (ds_ref[0, theirs, :].astype(F32) + ds_ref[1, theirs, :].astype(F32)).astype(BF16)
        b_copy(zt).start()
        bown[zt] = ds_ref[0, mine, :].astype(F32) + ds_ref[1, mine, :].astype(F32)

        @pl.when(step > 1)
        def _():
            pass_on(lax.rem(z + step - 1, nz))

    for j in range(2):
        kout_ref[j] = (kacc[j] * scale).astype(BF16)
        vout_ref[j] = vacc[j].astype(BF16)

    @pl.loop(1, nz + 1)
    def _(step):
        zt = lax.rem(z + step, nz)
        b_copy(zt).wait_recv()
        at = pl.ds(pl.multiple_of(zt * half, half), half)
        for hh in range(2):
            rows = slice(hh * n, (hh + 1) * n)
            bout_ref[hh, :, at] = (bown[zt, rows, :] + brecv[zt, rows, :].astype(F32)).astype(BF16)

    y_copy(z).wait_recv()
    qacc[z] += yin[z].astype(F32)

    @pl.loop(1, nz)
    def _(step):
        zt = lax.rem(z + nz - step, nz)
        z_copy(zt, zt).wait_recv()
        qacc[z] += zin[zt].astype(F32)

    for j in range(2):
        qout_ref[j] = (qacc[z, j].T * scale).astype(BF16)

    @pl.loop(0, nz)
    def _(zs):
        def sent(copy):
            copy.wait_send()

        for j in range(2):
            chain(zs, j, sent)
        y_copy(zs).wait_send()
        b_copy(zs).wait_send()

        @pl.when(zs != z)
        def _():
            z_copy(zs, z).wait_send()

    @pl.loop(1, ncols)
    def _(d):
        c = lax.rem(me + d, ncols)
        stat_copy(c).wait_send()
        fin_copy(c, me).wait_send()


def body(queries, keys, values, out_grad, key_mask, bias):
    n, slab_here, channels = queries.shape
    ncols = lax.axis_size("cols")
    nz = ncols // 2
    total = bias.shape[2]

    vmem = pl.BlockSpec(memory_space=pltpu.VMEM)
    dma = pltpu.SemaphoreType.DMA
    rows4 = 4 * n
    outs = pl.pallas_call(
        functools.partial(kernel, ncols),
        out_shape=(
            jax.ShapeDtypeStruct((2, n, channels), BF16),
            jax.ShapeDtypeStruct((2, n, channels), BF16),
            jax.ShapeDtypeStruct((2, n, channels), BF16),
            jax.ShapeDtypeStruct((2, n, total), BF16),
        ),
        in_specs=[vmem] * 5 + [pl.BlockSpec(memory_space=pl.ANY)],
        out_specs=(vmem,) * 4,
        scratch_shapes=[
            pltpu.VMEM((2, 2, total, channels), BF16),
            pltpu.VMEM((2, rows4, channels), BF16),
            pltpu.VMEM((2, channels, rows4), BF16),
            pltpu.VMEM((2, rows4, channels), BF16),
            pltpu.VMEM((2, n, n), F32),
            pltpu.VMEM((2, rows4, total), F32),
            pltpu.VMEM((2, rows4, total), F32),
            pltpu.VMEM((ncols, 3, 8, n), F32),
            pltpu.VMEM((ncols, 3, 8, n), F32),
            pltpu.VMEM((ncols, 2, 8, n), F32),
            pltpu.VMEM((2, rows4, 2 * n), BF16),
            pltpu.VMEM((2, rows4, 2 * n), BF16),
            pltpu.VMEM((2, n, channels), F32),
            pltpu.VMEM((2, n, channels), F32),
            pltpu.VMEM((2, channels, 2 * n), F32),
            pltpu.VMEM((nz, 2, channels, n), F32),
            pltpu.VMEM((nz, 2, channels, n), BF16),
            pltpu.VMEM((nz, 2, channels, n), BF16),
            pltpu.VMEM((nz, 2, channels, n), BF16),
            pltpu.VMEM((nz, 2 * n, 2 * n), F32),
            pltpu.VMEM((nz, 2 * n, 2 * n), BF16),
            pltpu.VMEM((nz, 2 * n, 2 * n), BF16),
            pltpu.VMEM(bias.shape, BF16),
            pltpu.VMEM((2 * n, channels), F32),
            dma((2, nz, 2)), dma((nz, 2)), dma((ncols, 2)),
            dma((ncols,)), dma((ncols,)), dma((ncols,)), dma((ncols,)),
            dma((nz,)), dma((nz,)), dma((nz,)), dma((nz,)), dma((nz,)), dma((nz,)), dma,
        ],
        compiler_params=pltpu.CompilerParams(
            collective_id=0, has_side_effects=True, vmem_limit_bytes=60 * 1024 * 1024),
    )(queries, keys, values, out_grad, key_mask.T, bias)
    query_grad, key_grad, value_grad, bias_grad = outs

    def back(a):
        return jnp.transpose(a, (1, 0, 2))

    return (back(query_grad), back(key_grad), back(value_grad), bias_grad)


def solution(mesh):
    block = P(("groups", "cols"), "rows", None)
    return jax.shard_map(
        body,
        mesh=mesh,
        in_specs=(block, block, block, block, P(("groups", "cols"), "rows"), P(None, ("groups", "cols"), None)),
        out_specs=(block, block, block, P("rows", ("groups", "cols"), None)),
        check_vma=False,
    )
```

```python
import functools

import jax
import jax.numpy as jnp
from jax import lax
from jax.experimental import pallas as pl
from jax.experimental.pallas import tpu as pltpu
from jax.sharding import PartitionSpec as P

HEAD_DIM = 32
MESH = pl.DeviceIdType.MESH
F32 = jnp.float32
BF16 = jnp.bfloat16


def dot_nt(a, b):
    return lax.dot_general(a, b, (((1,), (1,)), ((), ())), preferred_element_type=F32)


def dot_nn(a, b):
    return lax.dot_general(a, b, (((1,), (0,)), ((), ())), preferred_element_type=F32)


def kernel(
    ncols,
    q_in, k_in, v_in, do_in, mask_ref, bias_hbm,
    qout_ref, kacc, vacc, bout_ref,
    qg, k4, k4t, v4, pen, e_ref, dp_ref, stat, stin, fin,
    p_ref, ds_ref, qpart, qacc, ysbuf, yin, zin, bown, bsend, brecv, bias_ref, wide,
    zs_sem, ys_sem, g_sem, st_s, st_r, fin_s, fin_r, y_s, y_r, z_s, z_r, b_s, b_r, in_s,
):
    nz = ncols // 2
    scale = HEAD_DIM ** (-0.5)
    me = lax.axis_index("cols")
    core = lax.axis_index("rows")
    z = me // 2
    y = me % 2
    oy = 1 - y
    peer = z * 2 + oy
    n = k_in.shape[0]
    heads = 4

    def block_of(c):
        return pl.ds(pl.multiple_of(c * n, n), n)

    def slab(c, j):
        return qg.at[j, :, block_of(c), :]

    def column(j):
        return wide[pl.ds(j, n, stride=2), :]

    barrier = pltpu.get_barrier_semaphore()

    @pl.loop(1, ncols)
    def _(d):
        pl.semaphore_signal(barrier, inc=1, device_id={"cols": lax.rem(me + d, ncols)}, device_id_type=MESH)

    pl.semaphore_signal(barrier, inc=1, device_id={"rows": 1 - core}, device_id_type=MESH)

    bias_copy = pltpu.make_async_copy(bias_hbm, bias_ref, in_s)
    bias_copy.start()
    for at_kind, source in enumerate((q_in, do_in)):
        wide[...] = source[...].astype(F32).reshape(2 * n, 128)
        for j in range(2):
            qg[j, at_kind, block_of(me), :] = column(j).astype(BF16)
    pl.semaphore_wait(barrier, ncols)

    def up_copy(c, j):
        return pltpu.make_async_remote_copy(
            src_ref=slab(c, j), dst_ref=slab(c, j), send_sem=zs_sem.at[0, c // 2, j], recv_sem=g_sem.at[c, j],
            device_id={"cols": me + 2}, device_id_type=MESH)

    def down_copy(c, j):
        return pltpu.make_async_remote_copy(
            src_ref=slab(c, j), dst_ref=slab(c, j), send_sem=zs_sem.at[1, c // 2, j], recv_sem=g_sem.at[c, j],
            device_id={"cols": me - 2}, device_id_type=MESH)

    def side_copy(c, j):
        return pltpu.make_async_remote_copy(
            src_ref=slab(c, j), dst_ref=slab(c, j), send_sem=ys_sem.at[c // 2, j], recv_sem=g_sem.at[c, j],
            device_id={"cols": peer}, device_id_type=MESH)

    def chain_z(zs, j, act):
        c = zs * 2 + y

        @pl.when(jnp.logical_and(zs <= z, z < nz - 1))
        def _():
            act(up_copy(c, j))

        @pl.when(jnp.logical_and(zs >= z, z > 0))
        def _():
            act(down_copy(c, j))

    def chain(zs, j, act):
        chain_z(zs, j, act)
        act(side_copy(zs * 2 + y, j))

    def start(copy):
        copy.start()

    chain(z, 0, start)
    chain_z(z, 1, start)

    lane = lax.broadcasted_iota(jnp.int32, (n, 128), 1) // HEAD_DIM
    row = lax.broadcasted_iota(jnp.int32, (128, n), 0) // HEAD_DIM
    head_at = [lax.rem(hh + 2 * core, heads) for hh in range(heads)]
    wide[...] = v_in[...].astype(F32).reshape(2 * n, 128)
    for j in range(2):
        val = column(j)
        for hh in range(heads):
            rows = slice(hh * n, (hh + 1) * n)
            v4[j, rows, :] = jnp.where(lane == head_at[hh], val, 0.0).astype(BF16)
    wide[...] = k_in[...].astype(F32).reshape(2 * n, 128)
    for j in range(2):
        key = column(j)
        key_t = key.T
        for hh in range(heads):
            rows = slice(hh * n, (hh + 1) * n)
            k4[j, rows, :] = jnp.where(lane == head_at[hh], key, 0.0).astype(BF16)
            k4t[j, :, rows] = jnp.where(row == head_at[hh], key_t, 0.0).astype(BF16)
        pen[j] = jnp.broadcast_to(
            jnp.where(mask_ref[j:j + 1, :] > 0, 0.0, -1000000000.0).astype(F32), (n, n)).T
    kacc[...] = jnp.zeros_like(kacc)
    vacc[...] = jnp.zeros_like(vacc)
    bias_copy.wait()

    def stat_copy(j, c, slot):
        return pltpu.make_async_remote_copy(
            src_ref=stat.at[j, c], dst_ref=stin.at[j, slot], send_sem=st_s.at[j, c], recv_sem=st_r.at[j, slot],
            device_id={"cols": c}, device_id_type=MESH)

    def forward(c, j):
        at = block_of(c)
        x = dot_nt(k4[j], qg[j, 0, at, :])
        dp = dot_nt(v4[j], qg[j, 1, at, :])
        for hh in range(heads):
            rows = slice(hh * n, (hh + 1) * n)
            s = x[rows] * scale + bias_ref[head_at[hh], :, at].astype(F32) + pen[j]
            top = jnp.max(s, axis=0, keepdims=True)
            e = jnp.exp(s - top)
            e_ref[j, rows, at] = e
            dp_ref[j, rows, at] = dp[rows]
            stat[j, c, hh:hh + 1, :] = top
            stat[j, c, 4 + hh:5 + hh, :] = jnp.sum(e, axis=0, keepdims=True)
            stat[j, c, 8 + hh:9 + hh, :] = jnp.sum(e * dp[rows], axis=0, keepdims=True)

    short = jnp.minimum(z, nz - 1 - z)
    side = jnp.where(z < nz - 1 - z, 1, -1)

    def z_at(k):
        t = (k + 1) // 2
        near = z + t * (1 - 2 * (k % 2))
        return jnp.where(k <= 2 * short, near, z + side * (k - short))

    def fin_copy(j, c, slot):
        return pltpu.make_async_remote_copy(
            src_ref=fin.at[j, slot], dst_ref=fin.at[j, slot], send_sem=fin_s.at[j, c], recv_sem=fin_r.at[j, slot],
            device_id={"cols": c}, device_id_type=MESH)

    def combine(j):
        stin[j, me] = stat[j, me]

        @pl.loop(1, ncols)
        def _(d):
            c = lax.rem(me + d, ncols)
            stat_copy(j, c, c).wait_recv()

        top = stin[j, 0, 0:4, :]
        for c in range(1, ncols):
            top = jnp.maximum(top, stin[j, c, 0:4, :])
        total = jnp.zeros_like(top)
        for c in range(ncols):
            total = total + stin[j, c, 4:8, :] * jnp.exp(stin[j, c, 0:4, :] - top)
        lse = top + jnp.log(total)
        delta = jnp.zeros_like(top)
        for c in range(ncols):
            delta = delta + stin[j, c, 8:12, :] * jnp.exp(stin[j, c, 0:4, :] - lse)
        fin[j, me, 0:4, :] = lse
        fin[j, me, 4:8, :] = delta

        @pl.loop(1, ncols)
        def _(d):
            fin_copy(j, lax.rem(me + d, ncols), me).start()

    def gather(j):
        @pl.loop(0, nz)
        def _(k):
            zs = z_at(k)
            mine = zs * 2 + y
            other = z_at(k - 1) * 2 + oy

            @pl.when(k > 0)
            def _():
                side_copy(mine, j).wait_recv()
                chain(zs, j, start)

            if j == 1:

                @pl.when(k == nz - 1)
                def _():
                    combine(0)

            forward(mine, j)

            @pl.when(k > 0)
            def _():
                stat_copy(j, mine, me).start()
                side_copy(other, j).wait_recv()
                forward(other, j)
                stat_copy(j, other, me).start()

        if j == 0:
            side_copy(me, 1).start()
        last = z_at(nz - 1) * 2 + oy
        side_copy(last, j).wait_recv()
        forward(last, j)
        stat_copy(j, last, me).start()

    gather(0)
    gather(1)

    def y_copy(j, zt):
        return pltpu.make_async_remote_copy(
            src_ref=ysbuf.at[j, zt], dst_ref=yin.at[j, zt], send_sem=y_s.at[j, zt], recv_sem=y_r.at[j, zt],
            device_id={"cols": peer}, device_id_type=MESH)

    def z_copy(j, zt, slot):
        return pltpu.make_async_remote_copy(
            src_ref=yin.at[j, zt], dst_ref=zin.at[j, slot], send_sem=z_s.at[j, zt], recv_sem=z_r.at[j, slot],
            device_id={"cols": zt * 2 + y}, device_id_type=MESH)

    def b_copy(zt):
        return pltpu.make_async_remote_copy(
            src_ref=bsend.at[zt], dst_ref=brecv.at[zt], send_sem=b_s.at[zt], recv_sem=b_r.at[zt],
            device_id={"rows": 1 - core}, device_id_type=MESH)

    def wait_fin(j, c):
        @pl.when(c != me)
        def _():
            fin_copy(j, c, c).wait_recv()

    def pass_on(j, zt):
        y_copy(j, zt).wait_recv()
        yin[j, zt] = (qacc[j, zt] + yin[j, zt].astype(F32)).astype(BF16)
        z_copy(j, zt, z).start()

    half = 2 * n

    def backward(j):
        @pl.loop(1, nz + 1)
        def _(step):
            zt = lax.rem(z + step, nz)
            lo = zt * 2
            hi = zt * 2 + 1
            wait_fin(j, lo)
            wait_fin(j, hi)
            at = pl.ds(pl.multiple_of(zt * half, half), half)
            factor = jnp.concatenate(
                [jnp.exp(stat[j, c, 0:4, :] - fin[j, c, 0:4, :]) for c in (lo, hi)], axis=1)
            inner = jnp.concatenate([fin[j, c, 4:8, :] for c in (lo, hi)], axis=1)
            for hh in range(heads):
                rows = slice(hh * n, (hh + 1) * n)
                p = e_ref[j, rows, at] * factor[hh:hh + 1]
                p_ref[rows, :] = p.astype(BF16)
                ds = (p * (dp_ref[j, rows, at] - inner[hh:hh + 1])).astype(BF16)
                ds_ref[rows, :] = ds
                if j == 0:
                    e_ref[0, rows, at] = ds.astype(F32)
                else:
                    both = e_ref[0, rows, at] + ds.astype(F32)
                    if hh < 2:
                        bown[zt, rows, :] = both
                    else:
                        bsend[zt, (hh - 2) * n:(hh - 1) * n, :] = both.astype(BF16)
            if j == 1:
                b_copy(zt).start()
            qpart[...] = dot_nn(k4t[j], ds_ref[...])
            ysbuf[j, zt] = qpart[:, pl.ds(pl.multiple_of(oy * n, n), n)].astype(BF16)
            y_copy(j, zt).start()
            qacc[j, zt] = qpart[:, pl.ds(pl.multiple_of(y * n, n), n)]
            part_v = dot_nn(p_ref[...], qg[j, 1, at, :])
            part_k = dot_nn(ds_ref[...], qg[j, 0, at, :])
            pick_v = part_v[0:n]
            pick_k = part_k[0:n]
            for hh in range(1, heads):
                here = lane == head_at[hh]
                pick_v = jnp.where(here, part_v[hh * n:(hh + 1) * n], pick_v)
                pick_k = jnp.where(here, part_k[hh * n:(hh + 1) * n], pick_k)
            vacc[j] += pick_v
            kacc[j] += pick_k
            if j == 1:

                @pl.when(step > 1)
                def _():
                    pass_on(1, lax.rem(z + step - 1, nz))

    backward(0)
    combine(1)

    @pl.loop(1, nz)
    def _(step):
        pass_on(0, lax.rem(z + step, nz))

    backward(1)

    @pl.loop(1, nz + 1)
    def _(step):
        zt = lax.rem(z + step, nz)
        b_copy(zt).wait_recv()
        at = pl.ds(pl.multiple_of(zt * half, half), half)
        for hh in range(2):
            rows = slice(hh * n, (hh + 1) * n)
            bout_ref[hh, :, at] = (bown[zt, rows, :] + brecv[zt, rows, :].astype(F32)).astype(BF16)

    for j in range(2):
        y_copy(j, z).wait_recv()
        qout_ref[j] = qacc[j, z] + yin[j, z].astype(F32)

        @pl.loop(1, nz)
        def _(step):
            zt = lax.rem(z + nz - step, nz)
            z_copy(j, zt, zt).wait_recv()
            qout_ref[j] += zin[j, zt].astype(F32)

    @pl.loop(0, nz)
    def _(zs):
        def sent(copy):
            copy.wait_send()

        b_copy(zs).wait_send()
        for j in range(2):
            chain(zs, j, sent)
            y_copy(j, zs).wait_send()

            @pl.when(zs != z)
            def _():
                z_copy(j, zs, z).wait_send()

    @pl.loop(1, ncols)
    def _(d):
        c = lax.rem(me + d, ncols)
        for j in range(2):
            stat_copy(j, c, me).wait_send()
            fin_copy(j, c, me).wait_send()


def finish(q_ref, k_ref, v_ref, b_ref, qout_ref, kout_ref, vout_ref, bout_ref, wide):
    n = qout_ref.shape[0]
    scale = HEAD_DIM ** (-0.5)
    bout_ref[...] = b_ref[...]
    for out, column in (
        (qout_ref, lambda j: q_ref[j].T * scale),
        (kout_ref, lambda j: k_ref[j] * scale),
        (vout_ref, lambda j: v_ref[j]),
    ):
        for j in range(2):
            wide[pl.ds(j, n, stride=2), :] = column(j)
        out[...] = wide[...].reshape(n, 2, 128).astype(BF16)


def body(queries, keys, values, out_grad, key_mask, bias):
    n, slab_here, channels = queries.shape
    ncols = lax.axis_size("cols")
    nz = ncols // 2
    total = bias.shape[2]

    vmem = pl.BlockSpec(memory_space=pltpu.VMEM)
    dma = pltpu.SemaphoreType.DMA
    rows4 = 4 * n
    outs = pl.pallas_call(
        functools.partial(kernel, ncols),
        out_shape=(
            jax.ShapeDtypeStruct((2, n, channels), F32),
            jax.ShapeDtypeStruct((2, n, channels), F32),
            jax.ShapeDtypeStruct((2, n, channels), F32),
            jax.ShapeDtypeStruct((2, n, total), BF16),
        ),
        in_specs=[vmem] * 5 + [pl.BlockSpec(memory_space=pl.ANY)],
        out_specs=(vmem,) * 4,
        scratch_shapes=[
            pltpu.VMEM((2, 2, total, channels), BF16),
            pltpu.VMEM((2, rows4, channels), BF16),
            pltpu.VMEM((2, channels, rows4), BF16),
            pltpu.VMEM((2, rows4, channels), BF16),
            pltpu.VMEM((2, n, n), F32),
            pltpu.VMEM((2, rows4, total), F32),
            pltpu.VMEM((2, rows4, total), F32),
            pltpu.VMEM((2, ncols, 16, n), F32),
            pltpu.VMEM((2, ncols, 16, n), F32),
            pltpu.VMEM((2, ncols, 8, n), F32),
            pltpu.VMEM((rows4, 2 * n), BF16),
            pltpu.VMEM((rows4, 2 * n), BF16),
            pltpu.VMEM((channels, 2 * n), F32),
            pltpu.VMEM((2, nz, channels, n), F32),
            pltpu.VMEM((2, nz, channels, n), BF16),
            pltpu.VMEM((2, nz, channels, n), BF16),
            pltpu.VMEM((2, nz, channels, n), BF16),
            pltpu.VMEM((nz, 2 * n, 2 * n), F32),
            pltpu.VMEM((nz, 2 * n, 2 * n), BF16),
            pltpu.VMEM((nz, 2 * n, 2 * n), BF16),
            pltpu.VMEM(bias.shape, BF16),
            pltpu.VMEM((2 * n, channels), F32),
            dma((2, nz, 2)), dma((nz, 2)), dma((ncols, 2)),
            dma((2, ncols)), dma((2, ncols)), dma((2, ncols)), dma((2, ncols)),
            dma((2, nz)), dma((2, nz)), dma((2, nz)), dma((2, nz)), dma((nz,)), dma((nz,)), dma,
        ],
        compiler_params=pltpu.CompilerParams(
            collective_id=0, has_side_effects=True, vmem_limit_bytes=60 * 1024 * 1024),
    )(queries, keys, values, out_grad, key_mask.T, bias)
    block = jax.ShapeDtypeStruct((n, slab_here, channels), BF16)
    return pl.pallas_call(
        finish,
        out_shape=(block, block, block, jax.ShapeDtypeStruct((2, n, total), BF16)),
        in_specs=[vmem] * 4,
        out_specs=(vmem,) * 4,
        scratch_shapes=[pltpu.VMEM((2 * n, channels), F32)],
        compiler_params=pltpu.CompilerParams(vmem_limit_bytes=32 * 1024 * 1024),
    )(*outs)


def solution(mesh):
    block = P(("groups", "cols"), "rows", None)
    return jax.shard_map(
        body,
        mesh=mesh,
        in_specs=(block, block, block, block, P(("groups", "cols"), "rows"), P(None, ("groups", "cols"), None)),
        out_specs=(block, block, block, P("rows", ("groups", "cols"), None)),
        check_vma=False,
    )
```

```python
import functools

import jax
import jax.numpy as jnp
from jax import lax
from jax.experimental import pallas as pl
from jax.experimental.pallas import tpu as pltpu
from jax.sharding import PartitionSpec as P

HEAD_DIM = 32
MESH = pl.DeviceIdType.MESH
F32 = jnp.float32
BF16 = jnp.bfloat16


def dot_nt(a, b):
    return lax.dot_general(a, b, (((1,), (1,)), ((), ())), preferred_element_type=F32)


def dot_nn(a, b):
    return lax.dot_general(a, b, (((1,), (0,)), ((), ())), preferred_element_type=F32)


def kernel(
    ncols,
    q_in, k_in, v_in, do_in, mask_ref, bias_hbm,
    qout_ref, kacc, vacc, bout_ref,
    qg, k4, k4t, v4, pen, e_ref, dp_ref, stat, stin, fin,
    p_ref, ds_ref, qpart, qacc, ysbuf, yin, zin, bown, bsend, brecv, bias_ref, wide,
    zs_sem, ys_sem, g_sem, st_s, st_r, fin_s, fin_r, y_s, y_r, z_s, z_r, b_s, b_r, in_s,
):
    nz = ncols // 2
    scale = HEAD_DIM ** (-0.5)
    me = lax.axis_index("cols")
    core = lax.axis_index("rows")
    z = me // 2
    y = me % 2
    oy = 1 - y
    peer = z * 2 + oy
    n = k_in.shape[0]
    heads = 4

    def block_of(c):
        return pl.ds(pl.multiple_of(c * n, n), n)

    def slab(c, j):
        return qg.at[j, :, block_of(c), :]

    def column(j):
        return wide[pl.ds(j, n, stride=2), :]

    barrier = pltpu.get_barrier_semaphore()

    @pl.loop(1, ncols)
    def _(d):
        pl.semaphore_signal(barrier, inc=1, device_id={"cols": lax.rem(me + d, ncols)}, device_id_type=MESH)

    pl.semaphore_signal(barrier, inc=1, device_id={"rows": 1 - core}, device_id_type=MESH)

    bias_copy = pltpu.make_async_copy(bias_hbm, bias_ref, in_s)
    bias_copy.start()
    for at_kind, source in enumerate((q_in, do_in)):
        wide[...] = source[...].astype(F32).reshape(2 * n, 128)
        for j in range(2):
            qg[j, at_kind, block_of(me), :] = column(j).astype(BF16)
    pl.semaphore_wait(barrier, ncols)

    def up_copy(c, j):
        return pltpu.make_async_remote_copy(
            src_ref=slab(c, j), dst_ref=slab(c, j), send_sem=zs_sem.at[0, c // 2, j], recv_sem=g_sem.at[c, j],
            device_id={"cols": me + 2}, device_id_type=MESH)

    def down_copy(c, j):
        return pltpu.make_async_remote_copy(
            src_ref=slab(c, j), dst_ref=slab(c, j), send_sem=zs_sem.at[1, c // 2, j], recv_sem=g_sem.at[c, j],
            device_id={"cols": me - 2}, device_id_type=MESH)

    def side_copy(c, j):
        return pltpu.make_async_remote_copy(
            src_ref=slab(c, j), dst_ref=slab(c, j), send_sem=ys_sem.at[c // 2, j], recv_sem=g_sem.at[c, j],
            device_id={"cols": peer}, device_id_type=MESH)

    def chain(zs, j, act):
        c = zs * 2 + y

        @pl.when(jnp.logical_and(zs <= z, z < nz - 1))
        def _():
            act(up_copy(c, j))

        @pl.when(jnp.logical_and(zs >= z, z > 0))
        def _():
            act(down_copy(c, j))

        act(side_copy(c, j))

    def start(copy):
        copy.start()

    for j in range(2):
        chain(z, j, start)

    lane = lax.broadcasted_iota(jnp.int32, (n, 128), 1) // HEAD_DIM
    row = lax.broadcasted_iota(jnp.int32, (128, n), 0) // HEAD_DIM
    head_at = [lax.rem(hh + 2 * core, heads) for hh in range(heads)]
    wide[...] = v_in[...].astype(F32).reshape(2 * n, 128)
    for j in range(2):
        val = column(j)
        for hh in range(heads):
            rows = slice(hh * n, (hh + 1) * n)
            v4[j, rows, :] = jnp.where(lane == head_at[hh], val, 0.0).astype(BF16)
    wide[...] = k_in[...].astype(F32).reshape(2 * n, 128)
    for j in range(2):
        key = column(j)
        key_t = key.T
        for hh in range(heads):
            rows = slice(hh * n, (hh + 1) * n)
            k4[j, rows, :] = jnp.where(lane == head_at[hh], key, 0.0).astype(BF16)
            k4t[j, :, rows] = jnp.where(row == head_at[hh], key_t, 0.0).astype(BF16)
        pen[j] = jnp.broadcast_to(
            jnp.where(mask_ref[j:j + 1, :] > 0, 0.0, -1000000000.0).astype(F32), (n, n)).T
    kacc[...] = jnp.zeros_like(kacc)
    vacc[...] = jnp.zeros_like(vacc)
    bias_copy.wait()

    def stat_copy(c):
        return pltpu.make_async_remote_copy(
            src_ref=stat.at[c], dst_ref=stin.at[me], send_sem=st_s.at[c], recv_sem=st_r.at[me],
            device_id={"cols": c}, device_id_type=MESH)

    def forward(c, j):
        at = block_of(c)
        x = dot_nt(k4[j], qg[j, 0, at, :])
        dp = dot_nt(v4[j], qg[j, 1, at, :])
        for hh in range(heads):
            rows = slice(hh * n, (hh + 1) * n)
            s = x[rows] * scale + bias_ref[head_at[hh], :, at].astype(F32) + pen[j]
            top = jnp.max(s, axis=0, keepdims=True)
            e = jnp.exp(s - top)
            e_ref[j, rows, at] = e
            dp_ref[j, rows, at] = dp[rows]
            r = j * heads + hh
            stat[c, 0, r:r + 1, :] = top
            stat[c, 1, r:r + 1, :] = jnp.sum(e, axis=0, keepdims=True)
            stat[c, 2, r:r + 1, :] = jnp.sum(e * dp[rows], axis=0, keepdims=True)

    short = jnp.minimum(z, nz - 1 - z)
    side = jnp.where(z < nz - 1 - z, 1, -1)

    def z_at(k):
        t = (k + 1) // 2
        near = z + t * (1 - 2 * (k % 2))
        return jnp.where(k <= 2 * short, near, z + side * (k - short))

    @pl.loop(0, nz)
    def _(k):
        zs = z_at(k)
        mine = zs * 2 + y
        other = z_at(k - 1) * 2 + oy
        for j in range(2):

            @pl.when(k > 0)
            def _():
                side_copy(mine, j).wait_recv()
                chain(zs, j, start)

            forward(mine, j)
            if j == 1:

                @pl.when(k > 0)
                def _():
                    stat_copy(mine).start()

            @pl.when(k > 0)
            def _():
                side_copy(other, j).wait_recv()
                forward(other, j)
                if j == 1:
                    stat_copy(other).start()

    last = z_at(nz - 1) * 2 + oy
    for j in range(2):
        side_copy(last, j).wait_recv()
        forward(last, j)
    stat_copy(last).start()

    stin[me] = stat[me]

    @pl.loop(1, ncols)
    def _(d):
        c = lax.rem(me + d, ncols)
        pltpu.make_async_remote_copy(
            src_ref=stat.at[c], dst_ref=stin.at[c], send_sem=st_s.at[c], recv_sem=st_r.at[c],
            device_id={"cols": c}, device_id_type=MESH).wait_recv()

    top = stin[0, 0]
    for c in range(1, ncols):
        top = jnp.maximum(top, stin[c, 0])
    total = jnp.zeros_like(top)
    for c in range(ncols):
        total = total + stin[c, 1] * jnp.exp(stin[c, 0] - top)
    lse = top + jnp.log(total)
    delta = jnp.zeros_like(top)
    for c in range(ncols):
        delta = delta + stin[c, 2] * jnp.exp(stin[c, 0] - lse)
    fin[me, 0] = lse
    fin[me, 1] = delta

    def fin_copy(c, slot):
        return pltpu.make_async_remote_copy(
            src_ref=fin.at[slot], dst_ref=fin.at[slot], send_sem=fin_s.at[c], recv_sem=fin_r.at[slot],
            device_id={"cols": c}, device_id_type=MESH)

    @pl.loop(1, ncols)
    def _(d):
        fin_copy(lax.rem(me + d, ncols), me).start()

    def y_copy(zt):
        return pltpu.make_async_remote_copy(
            src_ref=ysbuf.at[zt], dst_ref=yin.at[zt], send_sem=y_s.at[zt], recv_sem=y_r.at[zt],
            device_id={"cols": peer}, device_id_type=MESH)

    def z_copy(zt, slot):
        return pltpu.make_async_remote_copy(
            src_ref=yin.at[zt], dst_ref=zin.at[slot], send_sem=z_s.at[zt], recv_sem=z_r.at[slot],
            device_id={"cols": zt * 2 + y}, device_id_type=MESH)

    def b_copy(zt):
        return pltpu.make_async_remote_copy(
            src_ref=bsend.at[zt], dst_ref=brecv.at[zt], send_sem=b_s.at[zt], recv_sem=b_r.at[zt],
            device_id={"rows": 1 - core}, device_id_type=MESH)

    def wait_fin(c):
        @pl.when(c != me)
        def _():
            fin_copy(c, c).wait_recv()

    def pass_on(zt):
        y_copy(zt).wait_recv()
        yin[zt] = (qacc[zt] + yin[zt].astype(F32)).astype(BF16)
        z_copy(zt, z).start()

    half = 2 * n

    @pl.loop(1, nz + 1)
    def _(step):
        zt = lax.rem(z + step, nz)
        wait_fin(zt * 2)
        wait_fin(zt * 2 + 1)
        at = pl.ds(pl.multiple_of(zt * half, half), half)
        shift0 = jnp.exp(stat[zt * 2, 0] - fin[zt * 2, 0])
        shift1 = jnp.exp(stat[zt * 2 + 1, 0] - fin[zt * 2 + 1, 0])
        factor = jnp.concatenate([shift0, shift1], axis=1)
        inner = jnp.concatenate([fin[zt * 2, 1], fin[zt * 2 + 1, 1]], axis=1)
        for j in range(2):
            for hh in range(heads):
                rows = slice(hh * n, (hh + 1) * n)
                r = j * heads + hh
                p = e_ref[j, rows, at] * factor[r:r + 1]
                p_ref[j, rows, :] = p.astype(BF16)
                ds_ref[j, rows, :] = (p * (dp_ref[j, rows, at] - inner[r:r + 1])).astype(BF16)
            qpart[j] = dot_nn(k4t[j], ds_ref[j])
        ysbuf[zt] = qpart[:, :, pl.ds(pl.multiple_of(oy * n, n), n)].astype(BF16)
        y_copy(zt).start()
        qacc[zt] = qpart[:, :, pl.ds(pl.multiple_of(y * n, n), n)]
        mine = slice(0, 2 * n)
        theirs = slice(2 * n, 4 * n)
        bsend[zt] = (ds_ref[0, theirs, :].astype(F32) + ds_ref[1, theirs, :].astype(F32)).astype(BF16)
        b_copy(zt).start()
        bown[zt] = ds_ref[0, mine, :].astype(F32) + ds_ref[1, mine, :].astype(F32)
        for j in range(2):
            part_v = dot_nn(p_ref[j], qg[j, 1, at, :])
            part_k = dot_nn(ds_ref[j], qg[j, 0, at, :])
            pick_v = part_v[0:n]
            pick_k = part_k[0:n]
            for hh in range(1, heads):
                here = lane == head_at[hh]
                pick_v = jnp.where(here, part_v[hh * n:(hh + 1) * n], pick_v)
                pick_k = jnp.where(here, part_k[hh * n:(hh + 1) * n], pick_k)
            vacc[j] += pick_v
            kacc[j] += pick_k

        @pl.when(step > 1)
        def _():
            pass_on(lax.rem(z + step - 1, nz))

    @pl.loop(1, nz + 1)
    def _(step):
        zt = lax.rem(z + step, nz)
        b_copy(zt).wait_recv()
        at = pl.ds(pl.multiple_of(zt * half, half), half)
        for hh in range(2):
            rows = slice(hh * n, (hh + 1) * n)
            bout_ref[hh, :, at] = (bown[zt, rows, :] + brecv[zt, rows, :].astype(F32)).astype(BF16)

    y_copy(z).wait_recv()
    qacc[z] += yin[z].astype(F32)

    @pl.loop(1, nz)
    def _(step):
        zt = lax.rem(z + nz - step, nz)
        z_copy(zt, zt).wait_recv()
        qacc[z] += zin[zt].astype(F32)

    for j in range(2):
        qout_ref[j] = qacc[z, j]

    @pl.loop(0, nz)
    def _(zs):
        def sent(copy):
            copy.wait_send()

        for j in range(2):
            chain(zs, j, sent)
        y_copy(zs).wait_send()
        b_copy(zs).wait_send()

        @pl.when(zs != z)
        def _():
            z_copy(zs, z).wait_send()

    @pl.loop(1, ncols)
    def _(d):
        c = lax.rem(me + d, ncols)
        stat_copy(c).wait_send()
        fin_copy(c, me).wait_send()


def finish(q_ref, k_ref, v_ref, b_ref, qout_ref, kout_ref, vout_ref, bout_ref, wide):
    n = qout_ref.shape[0]
    scale = HEAD_DIM ** (-0.5)
    bout_ref[...] = b_ref[...]
    for out, column in (
        (qout_ref, lambda j: q_ref[j].T * scale),
        (kout_ref, lambda j: k_ref[j] * scale),
        (vout_ref, lambda j: v_ref[j]),
    ):
        for j in range(2):
            wide[pl.ds(j, n, stride=2), :] = column(j)
        out[...] = wide[...].reshape(n, 2, 128).astype(BF16)


def body(queries, keys, values, out_grad, key_mask, bias):
    n, slab_here, channels = queries.shape
    ncols = lax.axis_size("cols")
    nz = ncols // 2
    total = bias.shape[2]

    vmem = pl.BlockSpec(memory_space=pltpu.VMEM)
    dma = pltpu.SemaphoreType.DMA
    rows4 = 4 * n
    outs = pl.pallas_call(
        functools.partial(kernel, ncols),
        out_shape=(
            jax.ShapeDtypeStruct((2, n, channels), F32),
            jax.ShapeDtypeStruct((2, n, channels), F32),
            jax.ShapeDtypeStruct((2, n, channels), F32),
            jax.ShapeDtypeStruct((2, n, total), BF16),
        ),
        in_specs=[vmem] * 5 + [pl.BlockSpec(memory_space=pl.ANY)],
        out_specs=(vmem,) * 4,
        scratch_shapes=[
            pltpu.VMEM((2, 2, total, channels), BF16),
            pltpu.VMEM((2, rows4, channels), BF16),
            pltpu.VMEM((2, channels, rows4), BF16),
            pltpu.VMEM((2, rows4, channels), BF16),
            pltpu.VMEM((2, n, n), F32),
            pltpu.VMEM((2, rows4, total), F32),
            pltpu.VMEM((2, rows4, total), F32),
            pltpu.VMEM((ncols, 3, 8, n), F32),
            pltpu.VMEM((ncols, 3, 8, n), F32),
            pltpu.VMEM((ncols, 2, 8, n), F32),
            pltpu.VMEM((2, rows4, 2 * n), BF16),
            pltpu.VMEM((2, rows4, 2 * n), BF16),
            pltpu.VMEM((2, channels, 2 * n), F32),
            pltpu.VMEM((nz, 2, channels, n), F32),
            pltpu.VMEM((nz, 2, channels, n), BF16),
            pltpu.VMEM((nz, 2, channels, n), BF16),
            pltpu.VMEM((nz, 2, channels, n), BF16),
            pltpu.VMEM((nz, 2 * n, 2 * n), F32),
            pltpu.VMEM((nz, 2 * n, 2 * n), BF16),
            pltpu.VMEM((nz, 2 * n, 2 * n), BF16),
            pltpu.VMEM(bias.shape, BF16),
            pltpu.VMEM((2 * n, channels), F32),
            dma((2, nz, 2)), dma((nz, 2)), dma((ncols, 2)),
            dma((ncols,)), dma((ncols,)), dma((ncols,)), dma((ncols,)),
            dma((nz,)), dma((nz,)), dma((nz,)), dma((nz,)), dma((nz,)), dma((nz,)), dma,
        ],
        compiler_params=pltpu.CompilerParams(
            collective_id=0, has_side_effects=True, vmem_limit_bytes=60 * 1024 * 1024),
    )(queries, keys, values, out_grad, key_mask.T, bias)
    block = jax.ShapeDtypeStruct((n, slab_here, channels), BF16)
    return pl.pallas_call(
        finish,
        out_shape=(block, block, block, jax.ShapeDtypeStruct((2, n, total), BF16)),
        in_specs=[vmem] * 4,
        out_specs=(vmem,) * 4,
        scratch_shapes=[pltpu.VMEM((2 * n, channels), F32)],
        compiler_params=pltpu.CompilerParams(vmem_limit_bytes=60 * 1024 * 1024),
    )(*outs)


def solution(mesh):
    block = P(("groups", "cols"), "rows", None)
    return jax.shard_map(
        body,
        mesh=mesh,
        in_specs=(block, block, block, block, P(("groups", "cols"), "rows"), P(None, ("groups", "cols"), None)),
        out_specs=(block, block, block, P("rows", ("groups", "cols"), None)),
        check_vma=False,
    )
```

```python
import functools

import jax
import jax.numpy as jnp
from jax import lax
from jax.experimental import pallas as pl
from jax.experimental.pallas import tpu as pltpu
from jax.sharding import PartitionSpec as P

HEAD_DIM = 32
MESH = pl.DeviceIdType.MESH
F32 = jnp.float32
BF16 = jnp.bfloat16


def dot_nt(a, b):
    return lax.dot_general(a, b, (((1,), (1,)), ((), ())), preferred_element_type=F32)


def dot_nn(a, b):
    return lax.dot_general(a, b, (((1,), (0,)), ((), ())), preferred_element_type=F32)


def kernel(
    ncols,
    q_in, k_in, v_in, do_in, mask_ref, bias_hbm,
    qout_ref, kacc, vacc, bout_ref,
    qg, k4, k4t, v4, pen, e_ref, dp_ref, stat, stin, fin,
    p_ref, ds_ref, qpart, qacc, ysbuf, yin, zin, bown, bsend, brecv, bias_ref, wide,
    zs_sem, ys_sem, g_sem, st_s, st_r, fin_s, fin_r, y_s, y_r, z_s, z_r, b_s, b_r, in_s,
):
    nz = ncols // 2
    scale = HEAD_DIM ** (-0.5)
    me = lax.axis_index("cols")
    core = lax.axis_index("rows")
    z = me // 2
    y = me % 2
    oy = 1 - y
    peer = z * 2 + oy
    n = k_in.shape[0]
    heads = 4

    def block_of(c):
        return pl.ds(pl.multiple_of(c * n, n), n)

    def slab(c, j):
        return qg.at[j, :, block_of(c), :]

    def column(j):
        return wide[pl.ds(j, n, stride=2), :]

    barrier = pltpu.get_barrier_semaphore()

    @pl.loop(1, ncols)
    def _(d):
        pl.semaphore_signal(barrier, inc=1, device_id={"cols": lax.rem(me + d, ncols)}, device_id_type=MESH)

    pl.semaphore_signal(barrier, inc=1, device_id={"rows": 1 - core}, device_id_type=MESH)

    bias_copy = pltpu.make_async_copy(bias_hbm, bias_ref, in_s)
    bias_copy.start()
    for at_kind, source in enumerate((q_in, do_in)):
        wide[...] = source[...].astype(F32).reshape(2 * n, 128)
        for j in range(2):
            qg[j, at_kind, block_of(me), :] = column(j).astype(BF16)
    pl.semaphore_wait(barrier, ncols)

    def up_copy(c, j):
        return pltpu.make_async_remote_copy(
            src_ref=slab(c, j), dst_ref=slab(c, j), send_sem=zs_sem.at[0, c // 2, j], recv_sem=g_sem.at[c, j],
            device_id={"cols": me + 2}, device_id_type=MESH)

    def down_copy(c, j):
        return pltpu.make_async_remote_copy(
            src_ref=slab(c, j), dst_ref=slab(c, j), send_sem=zs_sem.at[1, c // 2, j], recv_sem=g_sem.at[c, j],
            device_id={"cols": me - 2}, device_id_type=MESH)

    def side_copy(c, j):
        return pltpu.make_async_remote_copy(
            src_ref=slab(c, j), dst_ref=slab(c, j), send_sem=ys_sem.at[c // 2, j], recv_sem=g_sem.at[c, j],
            device_id={"cols": peer}, device_id_type=MESH)

    def chain(zs, j, act):
        c = zs * 2 + y
        act(side_copy(c, j))

        @pl.when(jnp.logical_and(zs <= z, z < nz - 1))
        def _():
            act(up_copy(c, j))

        @pl.when(jnp.logical_and(zs >= z, z > 0))
        def _():
            act(down_copy(c, j))

    def start(copy):
        copy.start()

    for j in range(2):
        chain(z, j, start)

    lane = lax.broadcasted_iota(jnp.int32, (n, 128), 1) // HEAD_DIM
    row = lax.broadcasted_iota(jnp.int32, (128, n), 0) // HEAD_DIM
    head_at = [lax.rem(hh + 2 * core, heads) for hh in range(heads)]
    wide[...] = v_in[...].astype(F32).reshape(2 * n, 128)
    for j in range(2):
        val = column(j)
        for hh in range(heads):
            rows = slice(hh * n, (hh + 1) * n)
            v4[j, rows, :] = jnp.where(lane == head_at[hh], val, 0.0).astype(BF16)
    wide[...] = k_in[...].astype(F32).reshape(2 * n, 128)
    for j in range(2):
        key = column(j)
        key_t = key.T
        for hh in range(heads):
            rows = slice(hh * n, (hh + 1) * n)
            k4[j, rows, :] = jnp.where(lane == head_at[hh], key, 0.0).astype(BF16)
            k4t[j, :, rows] = jnp.where(row == head_at[hh], key_t, 0.0).astype(BF16)
        pen[j] = jnp.broadcast_to(
            jnp.where(mask_ref[j:j + 1, :] > 0, 0.0, -1000000000.0).astype(F32), (n, n)).T
    kacc[...] = jnp.zeros_like(kacc)
    vacc[...] = jnp.zeros_like(vacc)
    bias_copy.wait()

    def stat_copy(c):
        return pltpu.make_async_remote_copy(
            src_ref=stat.at[c], dst_ref=stin.at[me], send_sem=st_s.at[c], recv_sem=st_r.at[me],
            device_id={"cols": c}, device_id_type=MESH)

    def forward(c, j):
        at = block_of(c)
        x = dot_nt(k4[j], qg[j, 0, at, :])
        dp = dot_nt(v4[j], qg[j, 1, at, :])
        for hh in range(heads):
            rows = slice(hh * n, (hh + 1) * n)
            s = x[rows] * scale + bias_ref[head_at[hh], :, at].astype(F32) + pen[j]
            top = jnp.max(s, axis=0, keepdims=True)
            e = jnp.exp(s - top)
            e_ref[j, rows, at] = e
            dp_ref[j, rows, at] = dp[rows]
            r = j * heads + hh
            stat[c, 0, r:r + 1, :] = top
            stat[c, 1, r:r + 1, :] = jnp.sum(e, axis=0, keepdims=True)
            stat[c, 2, r:r + 1, :] = jnp.sum(e * dp[rows], axis=0, keepdims=True)

    short = jnp.minimum(z, nz - 1 - z)
    side = jnp.where(z < nz - 1 - z, 1, -1)

    def z_at(k):
        t = (k + 1) // 2
        near = z + t * (1 - 2 * (k % 2))
        return jnp.where(k <= 2 * short, near, z + side * (k - short))

    @pl.loop(0, nz)
    def _(k):
        zs = z_at(k)
        mine = zs * 2 + y
        other = z_at(k - 1) * 2 + oy
        for j in range(2):

            @pl.when(k > 0)
            def _():
                side_copy(mine, j).wait_recv()
                chain(zs, j, start)

            forward(mine, j)
            if j == 1:

                @pl.when(k > 0)
                def _():
                    stat_copy(mine).start()

            @pl.when(k > 0)
            def _():
                side_copy(other, j).wait_recv()
                forward(other, j)
                if j == 1:
                    stat_copy(other).start()

    last = z_at(nz - 1) * 2 + oy
    for j in range(2):
        side_copy(last, j).wait_recv()
        forward(last, j)
    stat_copy(last).start()

    stin[me] = stat[me]

    @pl.loop(1, ncols)
    def _(d):
        c = lax.rem(me + d, ncols)
        pltpu.make_async_remote_copy(
            src_ref=stat.at[c], dst_ref=stin.at[c], send_sem=st_s.at[c], recv_sem=st_r.at[c],
            device_id={"cols": c}, device_id_type=MESH).wait_recv()

    top = stin[0, 0]
    for c in range(1, ncols):
        top = jnp.maximum(top, stin[c, 0])
    total = jnp.zeros_like(top)
    for c in range(ncols):
        total = total + stin[c, 1] * jnp.exp(stin[c, 0] - top)
    lse = top + jnp.log(total)
    delta = jnp.zeros_like(top)
    for c in range(ncols):
        delta = delta + stin[c, 2] * jnp.exp(stin[c, 0] - lse)
    fin[me, 0] = lse
    fin[me, 1] = delta

    def fin_copy(c, slot):
        return pltpu.make_async_remote_copy(
            src_ref=fin.at[slot], dst_ref=fin.at[slot], send_sem=fin_s.at[c], recv_sem=fin_r.at[slot],
            device_id={"cols": c}, device_id_type=MESH)

    @pl.loop(1, ncols)
    def _(d):
        fin_copy(lax.rem(me + d, ncols), me).start()

    def y_copy(zt):
        return pltpu.make_async_remote_copy(
            src_ref=ysbuf.at[zt], dst_ref=yin.at[zt], send_sem=y_s.at[zt], recv_sem=y_r.at[zt],
            device_id={"cols": peer}, device_id_type=MESH)

    def z_copy(zt, slot):
        return pltpu.make_async_remote_copy(
            src_ref=yin.at[zt], dst_ref=zin.at[slot], send_sem=z_s.at[zt], recv_sem=z_r.at[slot],
            device_id={"cols": zt * 2 + y}, device_id_type=MESH)

    def b_copy(zt):
        return pltpu.make_async_remote_copy(
            src_ref=bsend.at[zt], dst_ref=brecv.at[zt], send_sem=b_s.at[zt], recv_sem=b_r.at[zt],
            device_id={"rows": 1 - core}, device_id_type=MESH)

    def wait_fin(c):
        @pl.when(c != me)
        def _():
            fin_copy(c, c).wait_recv()

    def pass_on(zt):
        y_copy(zt).wait_recv()
        yin[zt] = (qacc[zt] + yin[zt].astype(F32)).astype(BF16)
        z_copy(zt, z).start()

    half = 2 * n

    @pl.loop(1, nz + 1)
    def _(step):
        zt = lax.rem(z + step, nz)
        wait_fin(zt * 2)
        wait_fin(zt * 2 + 1)
        at = pl.ds(pl.multiple_of(zt * half, half), half)
        shift0 = jnp.exp(stat[zt * 2, 0] - fin[zt * 2, 0])
        shift1 = jnp.exp(stat[zt * 2 + 1, 0] - fin[zt * 2 + 1, 0])
        factor = jnp.concatenate([shift0, shift1], axis=1)
        inner = jnp.concatenate([fin[zt * 2, 1], fin[zt * 2 + 1, 1]], axis=1)
        for j in range(2):
            for hh in range(heads):
                rows = slice(hh * n, (hh + 1) * n)
                r = j * heads + hh
                p = e_ref[j, rows, at] * factor[r:r + 1]
                p_ref[j, rows, :] = p.astype(BF16)
                ds_ref[j, rows, :] = (p * (dp_ref[j, rows, at] - inner[r:r + 1])).astype(BF16)
            qpart[j] = dot_nn(k4t[j], ds_ref[j])
        ysbuf[zt] = qpart[:, :, pl.ds(pl.multiple_of(oy * n, n), n)].astype(BF16)
        y_copy(zt).start()
        qacc[zt] = qpart[:, :, pl.ds(pl.multiple_of(y * n, n), n)]
        mine = slice(0, 2 * n)
        theirs = slice(2 * n, 4 * n)
        bsend[zt] = (ds_ref[0, theirs, :].astype(F32) + ds_ref[1, theirs, :].astype(F32)).astype(BF16)
        b_copy(zt).start()
        bown[zt] = ds_ref[0, mine, :].astype(F32) + ds_ref[1, mine, :].astype(F32)
        for j in range(2):
            part_v = dot_nn(p_ref[j], qg[j, 1, at, :])
            part_k = dot_nn(ds_ref[j], qg[j, 0, at, :])
            pick_v = part_v[0:n]
            pick_k = part_k[0:n]
            for hh in range(1, heads):
                here = lane == head_at[hh]
                pick_v = jnp.where(here, part_v[hh * n:(hh + 1) * n], pick_v)
                pick_k = jnp.where(here, part_k[hh * n:(hh + 1) * n], pick_k)
            vacc[j] += pick_v
            kacc[j] += pick_k

        @pl.when(step > 1)
        def _():
            pass_on(lax.rem(z + step - 1, nz))

    @pl.loop(1, nz + 1)
    def _(step):
        zt = lax.rem(z + step, nz)
        b_copy(zt).wait_recv()
        at = pl.ds(pl.multiple_of(zt * half, half), half)
        for hh in range(2):
            rows = slice(hh * n, (hh + 1) * n)
            bout_ref[hh, :, at] = (bown[zt, rows, :] + brecv[zt, rows, :].astype(F32)).astype(BF16)

    y_copy(z).wait_recv()
    qacc[z] += yin[z].astype(F32)

    @pl.loop(1, nz)
    def _(step):
        zt = lax.rem(z + nz - step, nz)
        z_copy(zt, zt).wait_recv()
        qacc[z] += zin[zt].astype(F32)

    for j in range(2):
        qout_ref[j] = qacc[z, j]

    @pl.loop(0, nz)
    def _(zs):
        def sent(copy):
            copy.wait_send()

        for j in range(2):
            chain(zs, j, sent)
        y_copy(zs).wait_send()
        b_copy(zs).wait_send()

        @pl.when(zs != z)
        def _():
            z_copy(zs, z).wait_send()

    @pl.loop(1, ncols)
    def _(d):
        c = lax.rem(me + d, ncols)
        stat_copy(c).wait_send()
        fin_copy(c, me).wait_send()


def finish(q_ref, k_ref, v_ref, b_ref, qout_ref, kout_ref, vout_ref, bout_ref, wide):
    n = qout_ref.shape[0]
    scale = HEAD_DIM ** (-0.5)
    bout_ref[...] = b_ref[...]
    for out, column in (
        (qout_ref, lambda j: q_ref[j].T * scale),
        (kout_ref, lambda j: k_ref[j] * scale),
        (vout_ref, lambda j: v_ref[j]),
    ):
        for j in range(2):
            wide[pl.ds(j, n, stride=2), :] = column(j)
        out[...] = wide[...].reshape(n, 2, 128).astype(BF16)


def body(queries, keys, values, out_grad, key_mask, bias):
    n, slab_here, channels = queries.shape
    ncols = lax.axis_size("cols")
    nz = ncols // 2
    total = bias.shape[2]

    vmem = pl.BlockSpec(memory_space=pltpu.VMEM)
    dma = pltpu.SemaphoreType.DMA
    rows4 = 4 * n
    outs = pl.pallas_call(
        functools.partial(kernel, ncols),
        out_shape=(
            jax.ShapeDtypeStruct((2, n, channels), F32),
            jax.ShapeDtypeStruct((2, n, channels), F32),
            jax.ShapeDtypeStruct((2, n, channels), F32),
            jax.ShapeDtypeStruct((2, n, total), BF16),
        ),
        in_specs=[vmem] * 5 + [pl.BlockSpec(memory_space=pl.ANY)],
        out_specs=(vmem,) * 4,
        scratch_shapes=[
            pltpu.VMEM((2, 2, total, channels), BF16),
            pltpu.VMEM((2, rows4, channels), BF16),
            pltpu.VMEM((2, channels, rows4), BF16),
            pltpu.VMEM((2, rows4, channels), BF16),
            pltpu.VMEM((2, n, n), F32),
            pltpu.VMEM((2, rows4, total), F32),
            pltpu.VMEM((2, rows4, total), F32),
            pltpu.VMEM((ncols, 3, 8, n), F32),
            pltpu.VMEM((ncols, 3, 8, n), F32),
            pltpu.VMEM((ncols, 2, 8, n), F32),
            pltpu.VMEM((2, rows4, 2 * n), BF16),
            pltpu.VMEM((2, rows4, 2 * n), BF16),
            pltpu.VMEM((2, channels, 2 * n), F32),
            pltpu.VMEM((nz, 2, channels, n), F32),
            pltpu.VMEM((nz, 2, channels, n), BF16),
            pltpu.VMEM((nz, 2, channels, n), BF16),
            pltpu.VMEM((nz, 2, channels, n), BF16),
            pltpu.VMEM((nz, 2 * n, 2 * n), F32),
            pltpu.VMEM((nz, 2 * n, 2 * n), BF16),
            pltpu.VMEM((nz, 2 * n, 2 * n), BF16),
            pltpu.VMEM(bias.shape, BF16),
            pltpu.VMEM((2 * n, channels), F32),
            dma((2, nz, 2)), dma((nz, 2)), dma((ncols, 2)),
            dma((ncols,)), dma((ncols,)), dma((ncols,)), dma((ncols,)),
            dma((nz,)), dma((nz,)), dma((nz,)), dma((nz,)), dma((nz,)), dma((nz,)), dma,
        ],
        compiler_params=pltpu.CompilerParams(
            collective_id=0, has_side_effects=True, vmem_limit_bytes=60 * 1024 * 1024),
    )(queries, keys, values, out_grad, key_mask.T, bias)
    block = jax.ShapeDtypeStruct((n, slab_here, channels), BF16)
    return pl.pallas_call(
        finish,
        out_shape=(block, block, block, jax.ShapeDtypeStruct((2, n, total), BF16)),
        in_specs=[vmem] * 4,
        out_specs=(vmem,) * 4,
        scratch_shapes=[pltpu.VMEM((2 * n, channels), F32)],
        compiler_params=pltpu.CompilerParams(vmem_limit_bytes=60 * 1024 * 1024),
    )(*outs)


def solution(mesh):
    block = P(("groups", "cols"), "rows", None)
    return jax.shard_map(
        body,
        mesh=mesh,
        in_specs=(block, block, block, block, P(("groups", "cols"), "rows"), P(None, ("groups", "cols"), None)),
        out_specs=(block, block, block, P("rows", ("groups", "cols"), None)),
        check_vma=False,
    )
```
